128 devices in a mesh: tm: 8 (over x, core), lata: 4 (over y), latb: 4 (over z).
Axes of the slice: x: 4, y: 4, z: 4, core: 2. Of those that a mesh axis runs over, the one named last changes fastest.
Arguments:
- images: float32 [32, 2048, 4096], P('tm', ('lata', 'latb')), may hold values from -24 to 24
- pair_order: int32 [512], replicated, may hold values from 0 to 511, each once
- legendre: bfloat16 [512, 1025, 2048], P(('tm', 'lata', 'latb')), may hold values from -0.125 to 0.125
Outputs:
- mode_series: float32 [512, 1025, 64], P(('tm', 'lata', 'latb'))
The draws below stay inside these ranges and needn't reach their ends.
Inputs may be any that keep to these rules, and one draw needn't show every extreme that they name: `pair_order`: each pair appears in exactly one slot.
All inputs are finite; a program needn't handle non-finite values.
Results may differ from the reference program's by a relative error of at most 0.0029.
Values may be sent and summed in bfloat16 or wider, within the bound.
No kernel may reach another device: no remote copies, remote signals or barrier semaphores. Data moves between devices by JAX's collectives and lax.ppermute only.
A program may use at most 192 MiB of HBM per device.

```python
import math
import jax
import jax.numpy as jnp
from jax import lax

NLAT = 2048
NLON = 4096
LMAX = 1023
TIME = 32
PAIRS = 512
ROWS = 1025


def draw_images(key, part):
    key = jax.random.fold_in(key, 7)
    first_key, second_key = jax.random.split(key)
    latitude = jnp.arange(NLAT, dtype=jnp.float32)[None, :, None]
    rising = 1.0 + 2.0 * latitude / (NLAT - 1)
    rough = jax.random.uniform(second_key, (TIME, NLAT, 1), jnp.float32, 0.5, 2.0)
    base = jnp.clip(jax.random.normal(first_key, (TIME, NLAT, NLON), jnp.float32), -4.0, 4.0)
    return (base * rising * rough).astype(jnp.float32)


def steps_of(own_key, extent, cuts, smallest, largest):
    def one(axis_at, blocks):
        heights = jax.random.uniform(jax.random.fold_in(jax.random.fold_in(own_key, 6), axis_at), (blocks,), jnp.float32, smallest / len(cuts), largest / len(cuts))
        return jnp.repeat(jnp.exp(heights), extent[axis_at] // blocks).reshape((-1,) + (1,) * (len(extent) - axis_at - 1))

    loudness = one(*cuts[0])
    for cut in cuts[1:]:
        loudness = loudness * one(*cut)
    return loudness


def gaussian(key, shape, deviation, most, cuts=(), kind=jnp.bfloat16):
    result = deviation * jax.random.normal(key, shape, jnp.float32)
    if cuts:
        result = result * steps_of(key, shape, cuts, -0.22, 0.18)
    return jnp.clip(result, -most, most).astype(kind)


def setup_inputs(seed: int = 0) -> dict:
    keys = jax.random.split(jax.random.key(seed), 4)
    images = draw_images(jax.random.fold_in(keys[3], 71), 0)
    pair_order = jax.random.permutation(keys[1], PAIRS).astype(jnp.int32)
    legendre = gaussian(keys[2], (PAIRS, ROWS, NLAT), NLAT ** -0.5, 0.125, ((0, 128),))
    return dict(images=images, pair_order=pair_order, legendre=legendre)


def reference(images, pair_order, legendre):
    field = images.astype(jnp.float32)
    power = jnp.sqrt(lax.optimization_barrier(jnp.sum(field * field, axis=(1, 2))) / (NLAT * NLON) + 1e-06)
    spec = jnp.fft.rfft(field, axis=2)[:, :, :LMAX + 1] / math.sqrt(NLON)
    parts = jnp.stack([jnp.real(spec), jnp.imag(spec)]) / power[None, :, None, None]
    parts = parts.astype(jnp.bfloat16)
    columns = jnp.transpose(parts, (3, 2, 0, 1)).reshape(LMAX + 1, NLAT, 2 * TIME)
    row_ids = jnp.arange(ROWS, dtype=jnp.int32)

    def one_slot(slot):
        first = pair_order[slot]
        second = (LMAX - first).astype(jnp.int32)
        joined = jnp.concatenate([jnp.take(columns, first, axis=0), jnp.take(columns, second, axis=0)], axis=1)
        block = jnp.dot(legendre[slot], joined, preferred_element_type=jnp.float32)
        keep = (row_ids < LMAX + 1 - first)[:, None]
        return jnp.where(keep, block[:, :2 * TIME], block[:, 2 * TIME:])
    return lax.map(one_slot, jnp.arange(PAIRS, dtype=jnp.int32))
```

```python
import math

import jax
import jax.numpy as jnp
import numpy as np
from jax import lax
from jax.experimental import pallas as pl
from jax.experimental.pallas import tpu as pltpu
from jax.sharding import PartitionSpec as P

NT = (((1,), (1,)), ((), ()))


def tables():
    q = np.arange(32)
    k = np.arange(256)

    def rows(freq, conj):
        angle = 2.0 * np.pi / 4096.0 * ((freq[:, None] * k[None, :]) % 4096)
        c, s = np.cos(angle) / 64.0, np.sin(angle) / 64.0
        re = np.concatenate([c, s], 1)
        im = np.concatenate([-s, c], 1)
        return re, (-im if conj else im)

    def real_rows(freq, second):
        angle = 2.0 * np.pi / 4096.0 * ((freq[:, None] * k[None, :]) % 4096)
        c, s = np.cos(angle) / 64.0, np.sin(angle) / 64.0
        zero = np.zeros_like(c)
        pair = (zero, c), (zero, -s)
        if not second:
            pair = (c, zero), (-s, zero)
        return [np.concatenate(p, 1) for p in pair]

    first, other = [], []
    for high in (0, 1):
        n = 63 - q if high else q
        first += list(real_rows(16 * n, False))
        other += list(rows(16 * n, False))
    for high in (0, 1):
        n = 63 - q if high else q
        first += list(real_rows(8 + 16 * n, True))
        other += list(rows(-16 * (n + 1), True))
    whole = np.stack([np.concatenate(first, 0), np.concatenate(other, 0)]).astype(np.float32)
    hi = whole.astype(jnp.bfloat16)
    lo = (whole - hi.astype(np.float32)).astype(jnp.bfloat16)
    angle = 2.0 * np.pi / 4096.0 * (np.arange(8)[:, None] * k[None, :])
    twiddle = np.stack([np.cos(angle), -np.sin(angle)], 1).reshape(16, 256).astype(np.float32)
    return np.concatenate([hi, lo], 2), twiddle


def rfft(x):
    n = len(x)
    if n == 2:
        return [(x[0] + x[1], None), (x[0] - x[1], None)]
    even, odd = rfft(x[0::2]), rfft(x[1::2])
    out = [None] * (n // 2 + 1)
    out[0] = (even[0][0] + odd[0][0], None)
    out[n // 2] = (even[0][0] - odd[0][0], None)
    for b in range(1, n // 4 + 1):
        er, ei = even[b]
        dr, di = odd[b]
        if 4 * b == n:
            out[b] = (er, -dr)
            continue
        c, s = math.cos(2 * math.pi * b / n), -math.sin(2 * math.pi * b / n)
        if 8 * b == n:
            tr, ti = (dr + di) * c, (di - dr) * c
        else:
            tr, ti = dr * c - di * s, dr * s + di * c
        out[b] = (er + tr, ei + ti)
        out[n // 2 - b] = (er - tr, ti - ei)
    return out


def fourier_kernel(order_ref, image_ref, matrix_ref, twiddle_ref, out_ref, square_ref, z_ref, natural_ref):
    step = pl.program_id(0)
    for t in range(2):

        def rows(i, total, t=t):
            at = pl.ds(pl.multiple_of(i * 16, 16), 16)
            to = pl.ds(pl.multiple_of(t * 128 + i * 16, 16), 16)
            for half in range(2):
                lanes = slice(half * 128, half * 128 + 128)
                x = [image_ref[t, at, b * 256 + half * 128 : b * 256 + half * 128 + 128] for b in range(16)]
                for v in x:
                    total = total + v * v
                bins = rfft(x)

                def put(g, part, value):
                    hi = value.astype(jnp.bfloat16)
                    lo = (value - hi.astype(jnp.float32)).astype(jnp.bfloat16)
                    z_ref[g, to, part * 256 + half * 128 : part * 256 + half * 128 + 128] = hi
                    z_ref[g, to, 512 + part * 256 + half * 128 : 512 + part * 256 + half * 128 + 128] = lo

                put(0, 0, bins[0][0])
                put(0, 1, bins[8][0])
                for g in range(1, 8):
                    re, im = bins[g]
                    c = twiddle_ref[2 * g : 2 * g + 1, lanes]
                    s = twiddle_ref[2 * g + 1 : 2 * g + 2, lanes]
                    put(g, 0, re * c - im * s)
                    put(g, 1, re * s + im * c)
            return total

        total = lax.fori_loop(0, 8, rows, jnp.zeros((16, 128), jnp.float32))
        square_ref[pl.ds(step * 2 + t, 1), :] = jnp.sum(total, axis=0, keepdims=True)

    for g in range(8):
        kind = 0 if g == 0 else 1
        got = lax.dot_general(matrix_ref[kind, :, :512], z_ref[g, :, :512], NT, preferred_element_type=jnp.float32)
        got += lax.dot_general(matrix_ref[kind, :, :512], z_ref[g, :, 512:], NT, preferred_element_type=jnp.float32)
        got += lax.dot_general(matrix_ref[kind, :, 512:], z_ref[g, :, :512], NT, preferred_element_type=jnp.float32)
        for which, residue in enumerate((g, 8 if g == 0 else 16 - g)):
            for w in range(2):
                slot = 15 - residue if w else residue
                for c in range(2):
                    block = got[((which * 2 + w) * 2 + c) * 32 : ((which * 2 + w) * 2 + c) * 32 + 32]
                    for t in range(2):
                        natural_ref[pl.ds(slot * 512 + w * 8 + c * 4 + step * 2 + t, 32, stride=16), :] = block[:, t * 128 : t * 128 + 128]

    @pl.when(step == 1)
    def _():
        def place(i, carry):
            for u in range(8):
                s = i * 8 + u
                p = order_ref[s]
                at = pl.multiple_of((p % 16) * 512 + (p // 16) * 16, 16)
                out_ref[pl.ds(pl.multiple_of(s * 16, 16), 16), :] = natural_ref[pl.ds(at, 16), :].astype(jnp.bfloat16)
            return carry

        lax.fori_loop(0, 64, place, 0)


def fourier(pair_order, images, matrix, twiddle):
    return pl.pallas_call(
        fourier_kernel,
        grid=(2,),
        out_shape=(jax.ShapeDtypeStruct((8192, 128), jnp.bfloat16), jax.ShapeDtypeStruct((4, 128), jnp.float32)),
        in_specs=[
            pl.BlockSpec(memory_space=pltpu.SMEM),
            pl.BlockSpec((2, 128, 4096), lambda i: (i, 0, 0)),
            pl.BlockSpec((2, 256, 1024), lambda i: (0, 0, 0)),
            pl.BlockSpec((16, 256), lambda i: (0, 0)),
        ],
        out_specs=(pl.BlockSpec((8192, 128), lambda i: (0, 0)), pl.BlockSpec((4, 128), lambda i: (0, 0))),
        scratch_shapes=[pltpu.VMEM((8, 256, 1024), jnp.bfloat16), pltpu.VMEM((8192, 128), jnp.float32)],
        compiler_params=pltpu.CompilerParams(vmem_limit_bytes=60 << 20),
        cost_estimate=pl.CostEstimate(flops=4 << 30, bytes_accessed=12 << 20, transcendentals=0),
    )(pair_order, images, matrix, twiddle)


def legendre_kernel(mine_ref, got_ref, mix_ref, scale_ref, legendre_ref, out_ref, column_ref):
    slot = pl.program_id(0)
    for band in range(16):
        for block in range(8):
            column_ref[block * 16 : block * 16 + 16, band * 128 : band * 128 + 128] = got_ref[
                block * 16 + band, pl.ds(pl.multiple_of(slot * 16, 16), 16), :
            ]
    columns = jnp.dot(mix_ref[...], column_ref[...], preferred_element_type=jnp.float32).astype(jnp.bfloat16)
    block = lax.dot_general(legendre_ref[0], columns, NT, preferred_element_type=jnp.float32)
    row = lax.broadcasted_iota(jnp.int32, (block.shape[0], 64), 0)
    kept = jnp.where(row <= 1023 - mine_ref[slot], block[:, :64], block[:, 64:])
    out_ref[0] = jnp.transpose(kept) * scale_ref[...]


def associated(mine, got, mix, scale, legendre):
    return pl.pallas_call(
        legendre_kernel,
        grid=(4,),
        out_shape=jax.ShapeDtypeStruct((4, 64, 1025), jnp.float32),
        in_specs=[
            pl.BlockSpec(memory_space=pltpu.SMEM),
            pl.BlockSpec((128, 64, 128), lambda i: (0, 0, 0)),
            pl.BlockSpec((128, 128), lambda i: (0, 0)),
            pl.BlockSpec((64, 1), lambda i: (0, 0)),
            pl.BlockSpec((1, 1025, 2048), lambda i: (i, 0, 0)),
        ],
        out_specs=pl.BlockSpec((1, 64, 1025), lambda i: (i, 0, 0)),
        scratch_shapes=[pltpu.VMEM((128, 2048), jnp.bfloat16)],
        compiler_params=pltpu.CompilerParams(vmem_limit_bytes=56 << 20),
        cost_estimate=pl.CostEstimate(flops=4 << 30, bytes_accessed=22 << 20, transcendentals=0),
    )(mine, got, mix, scale, legendre)


def shifted(value, axis, size, by):
    return lax.ppermute(value, axis, [(i, (i + by) % size) for i in range(size)])


def shards(images, pair_order, legendre):
    matrix, twiddle = tables()
    message, squares = fourier(pair_order, images, jnp.asarray(matrix), jnp.asarray(twiddle))
    axes = ("tm", "lata", "latb")
    got = lax.all_to_all(message.reshape(128, 64, 128), axes, split_axis=0, concat_axis=0, tiled=True)
    total = jnp.sum(squares, axis=1)
    for axis in ("latb", "lata"):
        total = total + sum(shifted(total, axis, 4, by) for by in range(1, 4))
    own = jnp.where(jnp.arange(8)[:, None] == lax.axis_index("tm"), total[None, :], 0.0)
    every = own + sum(shifted(own, "tm", 8, by) for by in range(1, 8))
    power = jnp.sqrt(every.reshape(32) / 8388608.0 + 1e-6)
    scale = jnp.tile(1.0 / power, 2).reshape(64, 1)
    mine = lax.dynamic_slice_in_dim(pair_order, lax.axis_index(axes) * 4, 4)
    mix = np.zeros((128, 128), np.float32)
    for block in range(8):
        for wc in range(4):
            for t in range(4):
                mix[wc * 32 + block * 4 + t, block * 16 + wc * 4 + t] = 1.0
    series = associated(mine, got, jnp.asarray(mix, jnp.bfloat16), scale, legendre)
    return jnp.transpose(series, (0, 2, 1))


def solution(mesh):
    in_specs = (P("tm", ("lata", "latb"), None), P(), P(("tm", "lata", "latb"), None, None))
    out_specs = P(("tm", "lata", "latb"), None, None)
    return jax.shard_map(shards, mesh=mesh, in_specs=in_specs, out_specs=out_specs, check_vma=False)
```

```python
import math

import jax
import jax.numpy as jnp
import numpy as np
from jax import lax
from jax.experimental import pallas as pl
from jax.experimental.pallas import tpu as pltpu
from jax.sharding import PartitionSpec as P

NT = (((1,), (1,)), ((), ()))


def tables():
    q = np.arange(32)
    k = np.arange(256)

    def rows(freq, conj):
        angle = 2.0 * np.pi / 4096.0 * ((freq[:, None] * k[None, :]) % 4096)
        c, s = np.cos(angle) / 64.0, np.sin(angle) / 64.0
        re = np.concatenate([c, s], 1)
        im = np.concatenate([-s, c], 1)
        return re, (-im if conj else im)

    def real_rows(freq, second):
        angle = 2.0 * np.pi / 4096.0 * ((freq[:, None] * k[None, :]) % 4096)
        c, s = np.cos(angle) / 64.0, np.sin(angle) / 64.0
        zero = np.zeros_like(c)
        pair = (zero, c), (zero, -s)
        if not second:
            pair = (c, zero), (-s, zero)
        return [np.concatenate(p, 1) for p in pair]

    first, other = [], []
    for high in (0, 1):
        n = 63 - q if high else q
        first += list(real_rows(16 * n, False))
        other += list(rows(16 * n, False))
    for high in (0, 1):
        n = 63 - q if high else q
        first += list(real_rows(8 + 16 * n, True))
        other += list(rows(-16 * (n + 1), True))
    whole = np.stack([np.concatenate(first, 0), np.concatenate(other, 0)]).astype(np.float32)
    hi = whole.astype(jnp.bfloat16)
    lo = (whole - hi.astype(np.float32)).astype(jnp.bfloat16)
    angle = 2.0 * np.pi / 4096.0 * (np.arange(8)[:, None] * k[None, :])
    twiddle = np.stack([np.cos(angle), -np.sin(angle)], 1).reshape(16, 256).astype(np.float32)
    return np.concatenate([hi, lo], 1), twiddle


def rfft(x):
    n = len(x)
    if n == 2:
        return [(x[0] + x[1], None), (x[0] - x[1], None)]
    even, odd = rfft(x[0::2]), rfft(x[1::2])
    out = [None] * (n // 2 + 1)
    out[0] = (even[0][0] + odd[0][0], None)
    out[n // 2] = (even[0][0] - odd[0][0], None)
    for b in range(1, n // 4 + 1):
        er, ei = even[b]
        dr, di = odd[b]
        if 4 * b == n:
            out[b] = (er, -dr)
            continue
        c, s = math.cos(2 * math.pi * b / n), -math.sin(2 * math.pi * b / n)
        if 8 * b == n:
            tr, ti = (dr + di) * c, (di - dr) * c
        else:
            tr, ti = dr * c - di * s, dr * s + di * c
        out[b] = (er + tr, ei + ti)
        out[n // 2 - b] = (er - tr, ti - ei)
    return out


STRIDE = 16


def natural_row(p_low):
    return p_low * 16 if STRIDE == 256 else p_low * 512


def rows_of(start):
    return pl.ds(start if isinstance(start, int) else pl.multiple_of(start, 16), 16)


def fourier_kernel(order_ref, image_ref, matrix_ref, twiddle_ref, out_ref, z_ref, natural_ref, square_ref):
    step = pl.program_id(0)

    def prepare(i, unit, totals):
        out = []
        for t in range(2):
            total = totals[t]
            at, to = rows_of(i * 16), rows_of(t * 128 + i * 16)
            for half in range(2):
                lanes = slice(half * 128, half * 128 + 128)
                x = [image_ref[t, at, b * 256 + half * 128 : b * 256 + half * 128 + 128] for b in range(16)]
                squares = [v * v for v in x]
                while len(squares) > 1:
                    squares = [u + v for u, v in zip(squares[0::2], squares[1::2])]
                total = total + squares[0]
                bins = rfft(x)

                def put(g, part, value):
                    hi = value.astype(jnp.bfloat16)
                    lo = (value - hi.astype(jnp.float32)).astype(jnp.bfloat16)
                    z_ref[unit, g, to, part * 256 + half * 128 : part * 256 + half * 128 + 128] = hi
                    z_ref[unit, g, to, 512 + part * 256 + half * 128 : 512 + part * 256 + half * 128 + 128] = lo

                put(0, 0, bins[0][0])
                put(0, 1, bins[8][0])
                for g in range(1, 8):
                    re, im = bins[g]
                    c = twiddle_ref[2 * g : 2 * g + 1, lanes]
                    s = twiddle_ref[2 * g + 1 : 2 * g + 2, lanes]
                    put(g, 0, re * c - im * s)
                    put(g, 1, re * s + im * c)
            out.append(total)
        return tuple(out)

    def transform(g, unit):
        kind = min(g, 1)
        both = lax.dot_general(matrix_ref[kind], z_ref[unit, g, :, :512], NT, preferred_element_type=jnp.float32)
        rest = lax.dot_general(matrix_ref[kind, :256], z_ref[unit, g, :, 512:], NT, preferred_element_type=jnp.float32)
        got = both[:256] + (both[256:] + rest)
        for which, residue in enumerate((g, 8 if g == 0 else 16 - g)):
            for w in range(2):
                low = 15 - residue if w else residue
                for c in range(2):
                    first = ((which * 2 + w) * 2 + c) * 32
                    for t in range(2):
                        row = low * 512 + w * 8 + c * 4 + unit * 2 + t
                        natural_ref[pl.ds(row, 32, stride=16), :] = got[first : first + 32, t * 128 : t * 128 + 128]

    def keep_squares(unit, totals):
        for t in range(2):
            square_ref[unit * 2 + t : unit * 2 + t + 1, :] = jnp.sum(totals[t], axis=0, keepdims=True)

    zero = jnp.zeros((16, 128), jnp.float32)

    @pl.when(step == 0)
    def _():
        keep_squares(0, lax.fori_loop(0, 8, lambda i, totals: prepare(i, 0, totals), (zero, zero)))

    @pl.when(step == 1)
    def _():
        totals = (zero, zero)
        for i in range(8):
            transform(i, 0)
            totals = prepare(i, 1, totals)
        keep_squares(1, totals)

    @pl.when(step == 2)
    def _():
        for g in range(8):
            transform(g, 1)
        sums = square_ref[...]
        high = sums.astype(jnp.bfloat16).astype(jnp.float32)
        tail = jnp.concatenate([high, sums - high], axis=0).astype(jnp.bfloat16)

        def place(d, carry):
            for u in range(4):
                p = order_ref[d * 4 + u]
                row = (p & 15) * 512 + lax.shift_right_logical(p, 4) * 16
                at = pl.multiple_of(row, 16)
                out_ref[d, u * 16 : u * 16 + 16, :] = natural_ref[pl.ds(at, 16), :].astype(jnp.bfloat16)
            out_ref[d, 64:72, :] = tail
            return carry

        lax.fori_loop(0, 128, place, 0, unroll=8)


def fourier(pair_order, images, matrix, twiddle):
    return pl.pallas_call(
        fourier_kernel,
        grid=(3,),
        out_shape=jax.ShapeDtypeStruct((128, 72, 128), jnp.bfloat16),
        in_specs=[
            pl.BlockSpec(memory_space=pltpu.SMEM),
            pl.BlockSpec((2, 128, 4096), lambda i: (jnp.minimum(i, 1), 0, 0)),
            pl.BlockSpec((2, 512, 512), lambda i: (0, 0, 0)),
            pl.BlockSpec((16, 256), lambda i: (0, 0)),
        ],
        out_specs=pl.BlockSpec((128, 72, 128), lambda i: (0, 0, 0)),
        scratch_shapes=[
            pltpu.VMEM((2, 8, 256, 1024), jnp.bfloat16),
            pltpu.VMEM((8192, 128), jnp.float32),
            pltpu.VMEM((4, 128), jnp.float32),
        ],
        compiler_params=pltpu.CompilerParams(vmem_limit_bytes=58 << 20),
        cost_estimate=pl.CostEstimate(flops=4 << 30, bytes_accessed=12 << 20, transcendentals=0),
    )(pair_order, images, matrix, twiddle)


PIECES = 4


def legendre_kernel(mine_ref, got_ref, legendre_ref, out_ref, weight_ref, column_ref, series_ref, in_sems, out_sems):
    def loads(slot):
        for piece in range(PIECES):
            rows = pl.ds(piece * 256, 257 if piece == PIECES - 1 else 256)
            yield pltpu.make_async_copy(legendre_ref.at[slot, rows], weight_ref.at[slot, rows], in_sems.at[slot, piece])

    def begin(slot):
        for copy in loads(slot):
            copy.start()

    begin(0)
    scales = []
    for block in range(8):
        total = got_ref[block * 16, 64:72, :].astype(jnp.float32)
        for band in range(1, 16):
            total = total + got_ref[block * 16 + band, 64:72, :].astype(jnp.float32)
        parts = jnp.sum(total, axis=1, keepdims=True)
        whole = parts + jnp.concatenate([parts[4:], parts[:4]], axis=0)
        scales.append(1.0 / jnp.sqrt(whole / 8388608.0 + 1e-6))
    for slot in range(4):
        for band in range(16):
            for block in range(8):
                column_ref[slot, block * 16 : block * 16 + 16, band * 128 : band * 128 + 128] = got_ref[
                    block * 16 + band, slot * 16 : slot * 16 + 16, :
                ]
    begin(1)

    def store(slot):
        return pltpu.make_async_copy(series_ref.at[slot], out_ref.at[slot], out_sems.at[slot])

    def work(slot, carry):
        @pl.when(slot < 2)
        def _():
            begin(slot + 2)

        for copy in loads(slot):
            copy.wait()
        product = lax.dot_general(weight_ref[slot], column_ref[slot], NT, preferred_element_type=jnp.float32)
        turned = jnp.transpose(product)
        keep = lax.broadcasted_iota(jnp.int32, (8, 1025), 1) <= 1023 - mine_ref[slot]
        for block in range(8):
            kept = jnp.where(keep, turned[block * 16 : block * 16 + 8], turned[block * 16 + 8 : block * 16 + 16])
            kept = kept * scales[block]
            series_ref[slot, block * 4 : block * 4 + 4, :] = kept[:4]
            series_ref[slot, 32 + block * 4 : 32 + block * 4 + 4, :] = kept[4:]
        store(slot).start()
        return carry

    lax.fori_loop(0, 4, work, 0)
    for slot in range(4):
        store(slot).wait()


def associated(mine, got, legendre):
    return pl.pallas_call(
        legendre_kernel,
        out_shape=jax.ShapeDtypeStruct((4, 64, 1025), jnp.float32),
        in_specs=[
            pl.BlockSpec(memory_space=pltpu.SMEM),
            pl.BlockSpec(memory_space=pltpu.VMEM),
            pl.BlockSpec(memory_space=pl.ANY),
        ],
        out_specs=pl.BlockSpec(memory_space=pl.ANY),
        scratch_shapes=[
            pltpu.VMEM((4, 1025, 2048), jnp.bfloat16),
            pltpu.VMEM((4, 128, 2048), jnp.bfloat16),
            pltpu.VMEM((4, 64, 1025), jnp.float32),
            pltpu.SemaphoreType.DMA((4, PIECES)),
            pltpu.SemaphoreType.DMA((4,)),
        ],
        compiler_params=pltpu.CompilerParams(vmem_limit_bytes=48 << 20),
        cost_estimate=pl.CostEstimate(flops=4 << 30, bytes_accessed=22 << 20, transcendentals=0),
    )(mine, got, legendre)


def shards(images, pair_order, legendre):
    matrix, twiddle = tables()
    message = fourier(pair_order, images, jnp.asarray(matrix), jnp.asarray(twiddle))
    axes = ("tm", "lata", "latb")
    got = lax.all_to_all(message, axes, split_axis=0, concat_axis=0, tiled=True)
    mine = lax.dynamic_slice_in_dim(pair_order, lax.axis_index(axes) * 4, 4)
    return jnp.transpose(associated(mine, got, legendre), (0, 2, 1))


def solution(mesh):
    in_specs = (P("tm", ("lata", "latb"), None), P(), P(("tm", "lata", "latb"), None, None))
    out_specs = P(("tm", "lata", "latb"), None, None)
    return jax.shard_map(shards, mesh=mesh, in_specs=in_specs, out_specs=out_specs, check_vma=False)
```

```python
import math

import jax
import jax.numpy as jnp
import numpy as np
from jax import lax
from jax.experimental import pallas as pl
from jax.experimental.pallas import tpu as pltpu
from jax.sharding import PartitionSpec as P

NT = (((1,), (1,)), ((), ()))


def tables():
    q = np.arange(32)
    k = np.arange(256)

    def rows(freq, sign):
        angle = 2.0 * np.pi / 4096.0 * ((freq[:, None] * k[None, :]) % 4096)
        c, s = np.cos(angle) / 64.0, np.sin(angle) / 64.0
        zero = np.zeros_like(c)
        if sign == 0:
            return np.concatenate([c, zero], 1), np.concatenate([-s, zero], 1)
        if sign == 8:
            return np.concatenate([zero, c], 1), np.concatenate([zero, -s], 1)
        return np.concatenate([c, sign * s], 1), np.concatenate([-s, sign * c], 1)

    groups = []
    for g in range(8):
        first = []
        for residue, sign in ((g, 1 if g else 0), (16 - g if g else 8, -1 if g else 8)):
            for high in (0, 1):
                first += list(rows(residue + 16 * (63 - q if high else q), sign))
        groups.append(np.concatenate(first, 0))
    whole = np.stack(groups).astype(np.float32)
    hi = whole.astype(jnp.bfloat16)
    lo = (whole - hi.astype(np.float32)).astype(jnp.bfloat16)
    return np.concatenate([hi, lo], 1)


def rfft(x):
    n = len(x)
    if n == 2:
        return [(x[0] + x[1], None), (x[0] - x[1], None)]
    even, odd = rfft(x[0::2]), rfft(x[1::2])
    out = [None] * (n // 2 + 1)
    out[0] = (even[0][0] + odd[0][0], None)
    out[n // 2] = (even[0][0] - odd[0][0], None)
    for b in range(1, n // 4 + 1):
        er, ei = even[b]
        dr, di = odd[b]
        if 4 * b == n:
            out[b] = (er, -dr)
            continue
        c, s = math.cos(2 * math.pi * b / n), -math.sin(2 * math.pi * b / n)
        if 8 * b == n:
            tr, ti = (dr + di) * c, (di - dr) * c
        else:
            tr, ti = dr * c - di * s, dr * s + di * c
        out[b] = (er + tr, ei + ti)
        out[n // 2 - b] = (er - tr, ti - ei)
    return out


STRIDE = 16


def natural_row(p_low):
    return p_low * 16 if STRIDE == 256 else p_low * 512


def fourier_kernel(
    order_ref, image_ref, matrix_ref, out_ref, field_ref, rows_ref, za_ref, zb_ref, natural_ref, square_ref, message_ref, in_sems, row_sem, out_sems
):
    z_refs = (za_ref, zb_ref)

    def load(image, piece):
        rows = pl.ds(pl.multiple_of(piece * 16, 16), 16)
        return pltpu.make_async_copy(image_ref.at[image, rows], field_ref.at[image, rows], in_sems.at[image, piece])

    def begin(image):
        for piece in range(8):
            load(image, piece).start()

    matrix_load = pltpu.make_async_copy(matrix_ref, rows_ref, row_sem)

    def prepare(image):
        z_ref = z_refs[image // 2]

        def piece(i, total):
            load(image, i).wait()
            at = pl.ds(pl.multiple_of(i * 16, 16), 16)
            to = pl.ds(pl.multiple_of(image % 2 * 128 + i * 16, 16), 16)
            for half in range(2):
                x = [field_ref[image, at, b * 256 + half * 128 : b * 256 + half * 128 + 128] for b in range(16)]
                squares = [v * v for v in x]
                while len(squares) > 1:
                    squares = [u + v for u, v in zip(squares[0::2], squares[1::2])]
                total = total + squares[0]
                bins = rfft(x)
                pairs = [(bins[0][0], bins[8][0])] + bins[1:8]
                for g in range(8):
                    for part in range(2):
                        value = pairs[g][part]
                        hi = value.astype(jnp.bfloat16)
                        lo = (value - hi.astype(jnp.float32)).astype(jnp.bfloat16)
                        lane = part * 256 + half * 128
                        z_ref[g, to, lane : lane + 128] = hi
                        z_ref[g, to, 512 + lane : 512 + lane + 128] = lo
            return total

        total = lax.fori_loop(0, 8, piece, jnp.zeros((16, 128), jnp.float32), unroll=2)
        square_ref[image : image + 1, :] = jnp.sum(total, axis=0, keepdims=True)

    def transform(g, unit):
        z_ref = z_refs[unit]
        both = lax.dot_general(rows_ref[g], z_ref[g, :, :512], NT, preferred_element_type=jnp.float32)
        rest = lax.dot_general(rows_ref[g, :256], z_ref[g, :, 512:], NT, preferred_element_type=jnp.float32)
        got = both[:256] + (both[256:] + rest)
        for which, residue in enumerate((g, 16 - g if g else 8)):
            for w in range(2):
                low = 15 - residue if w else residue
                for c in range(2):
                    first = ((which * 2 + w) * 2 + c) * 32
                    for t in range(2):
                        row = low * 768 + w * 8 + c * 4 + unit * 2 + t
                        natural_ref[pl.ds(row, 32, stride=24), :] = got[first : first + 32, t * 128 : t * 128 + 128]

    for image in range(4):
        begin(image)
    matrix_load.start()
    prepare(0)
    prepare(1)
    prepare(2)
    prepare(3)
    matrix_load.wait()
    for g in range(8):
        transform(g, 0)
    for g in range(8):
        transform(g, 1)
    sums = square_ref[...]
    high = sums.astype(jnp.bfloat16).astype(jnp.float32)
    tail = jnp.concatenate([high, sums - high], axis=0).astype(jnp.bfloat16)

    def send(part):
        rows = pl.ds(part * 32, 32)
        return pltpu.make_async_copy(message_ref.at[rows], out_ref.at[rows], out_sems.at[part])

    for part in range(4):

        def place(d, carry):
            for u in range(4):
                p = order_ref[d * 4 + u]
                at = pl.multiple_of((p & 15) * 768 + lax.shift_right_logical(p, 4) * 24, 8)
                message_ref[d, u * 16 : u * 16 + 16, :] = natural_ref[pl.ds(at, 16), :].astype(jnp.bfloat16)
            message_ref[d, 64:72, :] = tail
            return carry

        lax.fori_loop(part * 32, part * 32 + 32, place, 0, unroll=8)
        send(part).start()
    for part in range(4):
        send(part).wait()


def fourier(pair_order, images, matrix):
    return pl.pallas_call(
        fourier_kernel,
        out_shape=jax.ShapeDtypeStruct((128, 72, 128), jnp.bfloat16),
        in_specs=[
            pl.BlockSpec(memory_space=pltpu.SMEM),
            pl.BlockSpec(memory_space=pl.ANY),
            pl.BlockSpec(memory_space=pl.ANY),
        ],
        out_specs=pl.BlockSpec(memory_space=pl.ANY),
        scratch_shapes=[
            pltpu.VMEM((4, 128, 4096), jnp.float32),
            pltpu.VMEM((8, 512, 512), jnp.bfloat16),
            pltpu.VMEM((8, 256, 1024), jnp.bfloat16),
            pltpu.VMEM((8, 256, 1024), jnp.bfloat16),
            pltpu.VMEM((12288, 128), jnp.float32),
            pltpu.VMEM((4, 128), jnp.float32),
            pltpu.VMEM((128, 72, 128), jnp.bfloat16),
            pltpu.SemaphoreType.DMA((4, 8)),
            pltpu.SemaphoreType.DMA,
            pltpu.SemaphoreType.DMA((4,)),
        ],
        compiler_params=pltpu.CompilerParams(vmem_limit_bytes=60 << 20),
        cost_estimate=pl.CostEstimate(flops=4 << 30, bytes_accessed=14 << 20, transcendentals=0),
    )(pair_order, images, matrix)


PIECES = 4


def legendre_kernel(mine_ref, got_ref, legendre_ref, out_ref, weight_ref, column_ref, series_ref, in_sems, out_sems):
    def loads(slot):
        for piece in range(PIECES):
            rows = pl.ds(piece * 256, 257 if piece == PIECES - 1 else 256)
            yield pltpu.make_async_copy(legendre_ref.at[slot, rows], weight_ref.at[slot, rows], in_sems.at[slot, piece])

    def begin(slot):
        for copy in loads(slot):
            copy.start()

    begin(0)
    scales = []
    for block in range(8):
        total = got_ref[block * 16, 64:72, :].astype(jnp.float32)
        for band in range(1, 16):
            total = total + got_ref[block * 16 + band, 64:72, :].astype(jnp.float32)
        parts = jnp.sum(total, axis=1, keepdims=True)
        whole = parts + jnp.concatenate([parts[4:], parts[:4]], axis=0)
        scales.append(1.0 / jnp.sqrt(whole / 8388608.0 + 1e-6))
    for slot in range(4):
        for band in range(16):
            for block in range(8):
                column_ref[slot, block * 16 : block * 16 + 16, band * 128 : band * 128 + 128] = got_ref[
                    block * 16 + band, slot * 16 : slot * 16 + 16, :
                ]
    begin(1)

    def store(slot):
        return pltpu.make_async_copy(series_ref.at[slot], out_ref.at[slot], out_sems.at[slot])

    def work(slot, carry):
        @pl.when(slot < 2)
        def _():
            begin(slot + 2)

        for copy in loads(slot):
            copy.wait()
        product = lax.dot_general(weight_ref[slot], column_ref[slot], NT, preferred_element_type=jnp.float32)
        turned = jnp.transpose(product)
        keep = lax.broadcasted_iota(jnp.int32, (8, 1025), 1) <= 1023 - mine_ref[slot]
        for block in range(8):
            kept = jnp.where(keep, turned[block * 16 : block * 16 + 8], turned[block * 16 + 8 : block * 16 + 16])
            kept = kept * scales[block]
            series_ref[slot, block * 4 : block * 4 + 4, :] = kept[:4]
            series_ref[slot, 32 + block * 4 : 32 + block * 4 + 4, :] = kept[4:]
        store(slot).start()
        return carry

    lax.fori_loop(0, 4, work, 0)
    for slot in range(4):
        store(slot).wait()


def associated(mine, got, legendre):
    return pl.pallas_call(
        legendre_kernel,
        out_shape=jax.ShapeDtypeStruct((4, 64, 1025), jnp.float32),
        in_specs=[
            pl.BlockSpec(memory_space=pltpu.SMEM),
            pl.BlockSpec(memory_space=pltpu.VMEM),
            pl.BlockSpec(memory_space=pl.ANY),
        ],
        out_specs=pl.BlockSpec(memory_space=pl.ANY),
        scratch_shapes=[
            pltpu.VMEM((4, 1025, 2048), jnp.bfloat16),
            pltpu.VMEM((4, 128, 2048), jnp.bfloat16),
            pltpu.VMEM((4, 64, 1025), jnp.float32),
            pltpu.SemaphoreType.DMA((4, PIECES)),
            pltpu.SemaphoreType.DMA((4,)),
        ],
        compiler_params=pltpu.CompilerParams(vmem_limit_bytes=48 << 20),
        cost_estimate=pl.CostEstimate(flops=4 << 30, bytes_accessed=22 << 20, transcendentals=0),
    )(mine, got, legendre)


def shards(images, pair_order, legendre):
    message = fourier(pair_order, images, jnp.asarray(tables()))
    axes = ("tm", "lata", "latb")
    got = lax.all_to_all(message, axes, split_axis=0, concat_axis=0, tiled=True)
    mine = lax.dynamic_slice_in_dim(pair_order, lax.axis_index(axes) * 4, 4)
    return jnp.transpose(associated(mine, got, legendre), (0, 2, 1))


def solution(mesh):
    in_specs = (P("tm", ("lata", "latb"), None), P(), P(("tm", "lata", "latb"), None, None))
    out_specs = P(("tm", "lata", "latb"), None, None)
    return jax.shard_map(shards, mesh=mesh, in_specs=in_specs, out_specs=out_specs, check_vma=False)
```

```python
import math

import jax
import jax.numpy as jnp
import numpy as np
from jax import lax
from jax.experimental import pallas as pl
from jax.experimental.pallas import tpu as pltpu
from jax.sharding import PartitionSpec as P

NT = (((1,), (1,)), ((), ()))


def tables():
    q = np.arange(32)
    k = np.arange(256)

    def rows(freq, sign):
        angle = 2.0 * np.pi / 4096.0 * ((freq[:, None] * k[None, :]) % 4096)
        c, s = np.cos(angle) / 64.0, np.sin(angle) / 64.0
        zero = np.zeros_like(c)
        if sign == 0:
            return np.concatenate([c, zero], 1), np.concatenate([-s, zero], 1)
        if sign == 8:
            return np.concatenate([zero, c], 1), np.concatenate([zero, -s], 1)
        return np.concatenate([c, sign * s], 1), np.concatenate([-s, sign * c], 1)

    groups = []
    for g in range(8):
        first = []
        for residue, sign in ((g, 1 if g else 0), (16 - g if g else 8, -1 if g else 8)):
            for high in (0, 1):
                first += list(rows(residue + 16 * (63 - q if high else q), sign))
        groups.append(np.concatenate(first, 0))
    whole = np.stack(groups).astype(np.float32)
    hi = whole.astype(jnp.bfloat16)
    lo = (whole - hi.astype(np.float32)).astype(jnp.bfloat16)
    return np.concatenate([hi, lo], 1)


def rfft(x):
    n = len(x)
    if n == 2:
        return [(x[0] + x[1], None), (x[0] - x[1], None)]
    even, odd = rfft(x[0::2]), rfft(x[1::2])
    out = [None] * (n // 2 + 1)
    out[0] = (even[0][0] + odd[0][0], None)
    out[n // 2] = (even[0][0] - odd[0][0], None)
    for b in range(1, n // 4 + 1):
        er, ei = even[b]
        dr, di = odd[b]
        if 4 * b == n:
            out[b] = (er, -dr)
            continue
        c, s = math.cos(2 * math.pi * b / n), -math.sin(2 * math.pi * b / n)
        if 8 * b == n:
            tr, ti = (dr + di) * c, (di - dr) * c
        else:
            tr, ti = dr * c - di * s, dr * s + di * c
        out[b] = (er + tr, ei + ti)
        out[n // 2 - b] = (er - tr, ti - ei)
    return out


STRIDE = 16


def natural_row(p_low):
    return p_low * 16 if STRIDE == 256 else p_low * 512


def fourier_kernel(
    order_ref, image_ref, matrix_ref, out_ref, field_ref, rows_ref, za_ref, zb_ref, natural_ref, square_ref, message_ref, in_sems, row_sem, out_sems
):
    z_refs = (za_ref, zb_ref)

    def load(image, piece):
        rows = pl.ds(pl.multiple_of(piece * 16, 16), 16)
        return pltpu.make_async_copy(image_ref.at[image, rows], field_ref.at[image, rows], in_sems.at[image, piece])

    def begin(image):
        for piece in range(8):
            load(image, piece).start()

    matrix_load = pltpu.make_async_copy(matrix_ref, rows_ref, row_sem)

    def prepare(image):
        z_ref = z_refs[image // 2]

        def piece(i, total):
            load(image, i).wait()
            at = pl.ds(pl.multiple_of(i * 16, 16), 16)
            to = pl.ds(pl.multiple_of(image % 2 * 128 + i * 16, 16), 16)
            for half in range(2):
                x = [field_ref[image, at, b * 256 + half * 128 : b * 256 + half * 128 + 128] for b in range(16)]
                squares = [v * v for v in x]
                while len(squares) > 1:
                    squares = [u + v for u, v in zip(squares[0::2], squares[1::2])]
                total = total + squares[0]
                bins = rfft(x)
                pairs = [(bins[0][0], bins[8][0])] + bins[1:8]
                for g in range(8):
                    for part in range(2):
                        value = pairs[g][part]
                        hi = value.astype(jnp.bfloat16)
                        lo = (value - hi.astype(jnp.float32)).astype(jnp.bfloat16)
                        lane = part * 256 + half * 128
                        z_ref[g, to, lane : lane + 128] = hi
                        z_ref[g, to, 512 + lane : 512 + lane + 128] = lo
            return total

        total = lax.fori_loop(0, 8, piece, jnp.zeros((16, 128), jnp.float32), unroll=2)
        square_ref[image : image + 1, :] = jnp.sum(total, axis=0, keepdims=True)

    def transform(g, unit):
        z_ref = z_refs[unit]
        both = lax.dot_general(rows_ref[g], z_ref[g, :, :512], NT, preferred_element_type=jnp.float32)
        rest = lax.dot_general(rows_ref[g, :256], z_ref[g, :, 512:], NT, preferred_element_type=jnp.float32)
        got = both[:256] + (both[256:] + rest)
        for which, residue in enumerate((g, 16 - g if g else 8)):
            for w in range(2):
                low = 15 - residue if w else residue
                for c in range(2):
                    first = ((which * 2 + w) * 2 + c) * 32
                    for t in range(2):
                        row = low * 768 + w * 8 + c * 4 + unit * 2 + t
                        natural_ref[pl.ds(row, 32, stride=24), :] = got[first : first + 32, t * 128 : t * 128 + 128]

    for image in range(4):
        begin(image)
    matrix_load.start()
    prepare(0)
    prepare(1)
    prepare(2)
    prepare(3)
    matrix_load.wait()
    for g in range(8):
        transform(g, 0)
    for g in range(8):
        transform(g, 1)
    lane = lax.broadcasted_iota(jnp.int32, (4, 128), 1)
    image = lax.broadcasted_iota(jnp.int32, (4, 128), 0)
    sums = jnp.sum(square_ref[...], axis=1, keepdims=True)
    sums = jnp.sum(jnp.where(lane == image, sums, 0.0), axis=0, keepdims=True)
    high = sums.astype(jnp.bfloat16).astype(jnp.float32)
    tail = jnp.concatenate([high, sums - high], axis=0).astype(jnp.bfloat16)

    def send(part):
        rows = pl.ds(part * 32, 32)
        return pltpu.make_async_copy(message_ref.at[rows], out_ref.at[rows], out_sems.at[part])

    for part in range(4):

        def place(d, carry):
            for u in range(4):
                p = order_ref[d * 4 + u]
                at = pl.multiple_of((p & 15) * 768 + lax.shift_right_logical(p, 4) * 24, 8)
                message_ref[d, u * 8 : u * 8 + 8, :, :] = natural_ref[pl.ds(at, 16), :].astype(jnp.bfloat16).reshape(8, 2, 128)
            message_ref[d, 32, :, :] = tail
            return carry

        lax.fori_loop(part * 32, part * 32 + 32, place, 0, unroll=8)
        send(part).start()
    for part in range(4):
        send(part).wait()


def fourier(pair_order, images, matrix):
    return pl.pallas_call(
        fourier_kernel,
        out_shape=jax.ShapeDtypeStruct((128, 33, 2, 128), jnp.bfloat16),
        in_specs=[
            pl.BlockSpec(memory_space=pltpu.SMEM),
            pl.BlockSpec(memory_space=pl.ANY),
            pl.BlockSpec(memory_space=pl.ANY),
        ],
        out_specs=pl.BlockSpec(memory_space=pl.ANY),
        scratch_shapes=[
            pltpu.VMEM((4, 128, 4096), jnp.float32),
            pltpu.VMEM((8, 512, 512), jnp.bfloat16),
            pltpu.VMEM((8, 256, 1024), jnp.bfloat16),
            pltpu.VMEM((8, 256, 1024), jnp.bfloat16),
            pltpu.VMEM((12288, 128), jnp.float32),
            pltpu.VMEM((4, 128), jnp.float32),
            pltpu.VMEM((128, 33, 2, 128), jnp.bfloat16),
            pltpu.SemaphoreType.DMA((4, 8)),
            pltpu.SemaphoreType.DMA,
            pltpu.SemaphoreType.DMA((4,)),
        ],
        compiler_params=pltpu.CompilerParams(vmem_limit_bytes=60 << 20),
        cost_estimate=pl.CostEstimate(flops=4 << 30, bytes_accessed=14 << 20, transcendentals=0),
    )(pair_order, images, matrix)


PIECES = 4


def legendre_kernel(mine_ref, got_ref, legendre_ref, out_ref, weight_ref, column_ref, series_ref, in_sems, out_sems):
    def loads(slot):
        for piece in range(PIECES):
            rows = pl.ds(piece * 256, 257 if piece == PIECES - 1 else 256)
            yield pltpu.make_async_copy(legendre_ref.at[slot, rows], weight_ref.at[slot, rows], in_sems.at[slot, piece])

    def begin(slot):
        for copy in loads(slot):
            copy.start()

    begin(0)
    lanes = lax.broadcasted_iota(jnp.int32, (8, 128), 1)
    images = lax.broadcasted_iota(jnp.int32, (8, 128), 0) & 3
    scales = []
    for block in range(8):
        total = got_ref[block * 16, 32, :, :].astype(jnp.float32)
        for band in range(1, 16):
            total = total + got_ref[block * 16 + band, 32, :, :].astype(jnp.float32)
        both = jnp.broadcast_to(total[0:1] + total[1:2], (8, 128))
        whole = jnp.sum(jnp.where(lanes == images, both, 0.0), axis=1, keepdims=True)
        scales.append(1.0 / jnp.sqrt(whole / 8388608.0 + 1e-6))
    for slot in range(4):
        for band in range(16):
            for block in range(8):
                column_ref[slot, block * 16 : block * 16 + 16, band * 128 : band * 128 + 128] = got_ref[
                    block * 16 + band, slot * 8 : slot * 8 + 8, :, :
                ].reshape(16, 128)
    begin(1)

    def store(slot):
        return pltpu.make_async_copy(series_ref.at[slot], out_ref.at[slot], out_sems.at[slot])

    def work(slot, carry):
        @pl.when(slot < 2)
        def _():
            begin(slot + 2)

        for copy in loads(slot):
            copy.wait()
        product = lax.dot_general(weight_ref[slot], column_ref[slot], NT, preferred_element_type=jnp.float32)
        turned = jnp.transpose(product)
        keep = lax.broadcasted_iota(jnp.int32, (8, 1025), 1) <= 1023 - mine_ref[slot]
        for block in range(8):
            kept = jnp.where(keep, turned[block * 16 : block * 16 + 8], turned[block * 16 + 8 : block * 16 + 16])
            kept = kept * scales[block]
            series_ref[slot, block * 4 : block * 4 + 4, :] = kept[:4]
            series_ref[slot, 32 + block * 4 : 32 + block * 4 + 4, :] = kept[4:]
        store(slot).start()
        return carry

    lax.fori_loop(0, 4, work, 0)
    for slot in range(4):
        store(slot).wait()


def associated(mine, got, legendre):
    return pl.pallas_call(
        legendre_kernel,
        out_shape=jax.ShapeDtypeStruct((4, 64, 1025), jnp.float32),
        in_specs=[
            pl.BlockSpec(memory_space=pltpu.SMEM),
            pl.BlockSpec(memory_space=pltpu.VMEM),
            pl.BlockSpec(memory_space=pl.ANY),
        ],
        out_specs=pl.BlockSpec(memory_space=pl.ANY),
        scratch_shapes=[
            pltpu.VMEM((4, 1025, 2048), jnp.bfloat16),
            pltpu.VMEM((4, 128, 2048), jnp.bfloat16),
            pltpu.VMEM((4, 64, 1025), jnp.float32),
            pltpu.SemaphoreType.DMA((4, PIECES)),
            pltpu.SemaphoreType.DMA((4,)),
        ],
        compiler_params=pltpu.CompilerParams(vmem_limit_bytes=48 << 20),
        cost_estimate=pl.CostEstimate(flops=4 << 30, bytes_accessed=22 << 20, transcendentals=0),
    )(mine, got, legendre)


def shards(images, pair_order, legendre):
    message = fourier(pair_order, images, jnp.asarray(tables()))
    axes = ("tm", "lata", "latb")
    got = lax.all_to_all(message, axes, split_axis=0, concat_axis=0, tiled=True)
    mine = lax.dynamic_slice_in_dim(pair_order, lax.axis_index(axes) * 4, 4)
    return jnp.transpose(associated(mine, got, legendre), (0, 2, 1))


def solution(mesh):
    in_specs = (P("tm", ("lata", "latb"), None), P(), P(("tm", "lata", "latb"), None, None))
    out_specs = P(("tm", "lata", "latb"), None, None)
    return jax.shard_map(shards, mesh=mesh, in_specs=in_specs, out_specs=out_specs, check_vma=False)
```

```python
import math

import jax
import jax.numpy as jnp
import numpy as np
from jax import lax
from jax.experimental import pallas as pl
from jax.experimental.pallas import tpu as pltpu
from jax.sharding import PartitionSpec as P

NT = (((1,), (1,)), ((), ()))


def tables():
    q = np.arange(32)
    k = np.arange(256)

    def rows(freq, sign):
        angle = 2.0 * np.pi / 4096.0 * ((freq[:, None] * k[None, :]) % 4096)
        c, s = np.cos(angle) / 64.0, np.sin(angle) / 64.0
        zero = np.zeros_like(c)
        if sign == 0:
            return np.concatenate([c, zero], 1), np.concatenate([-s, zero], 1)
        if sign == 8:
            return np.concatenate([zero, c], 1), np.concatenate([zero, -s], 1)
        return np.concatenate([c, sign * s], 1), np.concatenate([-s, sign * c], 1)

    groups = []
    for g in range(8):
        first = []
        for residue, sign in ((g, 1 if g else 0), (16 - g if g else 8, -1 if g else 8)):
            for high in (0, 1):
                first += list(rows(residue + 16 * (63 - q if high else q), sign))
        groups.append(np.concatenate(first, 0))
    whole = np.stack(groups).astype(np.float32)
    hi = whole.astype(jnp.bfloat16)
    lo = (whole - hi.astype(np.float32)).astype(jnp.bfloat16)
    return np.concatenate([hi, lo], 1)


def rfft(x):
    n = len(x)
    if n == 2:
        return [(x[0] + x[1], None), (x[0] - x[1], None)]
    even, odd = rfft(x[0::2]), rfft(x[1::2])
    out = [None] * (n // 2 + 1)
    out[0] = (even[0][0] + odd[0][0], None)
    out[n // 2] = (even[0][0] - odd[0][0], None)
    for b in range(1, n // 4 + 1):
        er, ei = even[b]
        dr, di = odd[b]
        if 4 * b == n:
            out[b] = (er, -dr)
            continue
        c, s = math.cos(2 * math.pi * b / n), -math.sin(2 * math.pi * b / n)
        if 8 * b == n:
            tr, ti = (dr + di) * c, (di - dr) * c
        else:
            tr, ti = dr * c - di * s, dr * s + di * c
        out[b] = (er + tr, ei + ti)
        out[n // 2 - b] = (er - tr, ti - ei)
    return out


STRIDE = 16


def natural_row(p_low):
    return p_low * 16 if STRIDE == 256 else p_low * 512


def fourier_kernel(
    pair_ref, image_ref, matrix_ref, out_ref, order_ref, field_ref, rows_ref, za_ref, zb_ref, natural_ref, square_ref, message_ref, in_sems, row_sem, order_sem, out_sems
):
    z_refs = (za_ref, zb_ref)

    def load(image, piece):
        rows = pl.ds(pl.multiple_of(piece * 16, 16), 16)
        return pltpu.make_async_copy(image_ref.at[image, rows], field_ref.at[image, rows], in_sems.at[image, piece])

    def begin(image):
        for piece in range(8):
            load(image, piece).start()

    matrix_load = pltpu.make_async_copy(matrix_ref, rows_ref, row_sem)

    def prepare(image):
        z_ref = z_refs[image // 2]

        def piece(i, total):
            load(image, i).wait()
            at = pl.ds(pl.multiple_of(i * 16, 16), 16)
            to = pl.ds(pl.multiple_of(image % 2 * 128 + i * 16, 16), 16)
            for half in range(2):
                x = [field_ref[image, at, b * 256 + half * 128 : b * 256 + half * 128 + 128] for b in range(16)]
                squares = [v * v for v in x]
                while len(squares) > 1:
                    squares = [u + v for u, v in zip(squares[0::2], squares[1::2])]
                total = total + squares[0]
                bins = rfft(x)
                pairs = [(bins[0][0], bins[8][0])] + bins[1:8]
                for g in range(8):
                    for part in range(2):
                        value = pairs[g][part]
                        hi = value.astype(jnp.bfloat16)
                        lo = (value - hi.astype(jnp.float32)).astype(jnp.bfloat16)
                        lane = part * 256 + half * 128
                        z_ref[g, to, lane : lane + 128] = hi
                        z_ref[g, to, 512 + lane : 512 + lane + 128] = lo
            return total

        total = lax.fori_loop(0, 8, piece, jnp.zeros((16, 128), jnp.float32), unroll=2)
        square_ref[image : image + 1, :] = jnp.sum(total, axis=0, keepdims=True)

    def transform(g, unit):
        z_ref = z_refs[unit]
        both = lax.dot_general(rows_ref[g], z_ref[g, :, :512], NT, preferred_element_type=jnp.float32)
        rest = lax.dot_general(rows_ref[g, :256], z_ref[g, :, 512:], NT, preferred_element_type=jnp.float32)
        got = both[:256] + (both[256:] + rest)
        for which, residue in enumerate((g, 16 - g if g else 8)):
            for w in range(2):
                low = 15 - residue if w else residue
                for c in range(2):
                    first = ((which * 2 + w) * 2 + c) * 32
                    for t in range(2):
                        row = low * 768 + w * 8 + c * 4 + unit * 2 + t
                        natural_ref[pl.ds(row, 32, stride=24), :] = got[first : first + 32, t * 128 : t * 128 + 128]

    for image in range(4):
        begin(image)
    matrix_load.start()
    order_load = pltpu.make_async_copy(pair_ref, order_ref, order_sem)
    order_load.start()
    prepare(0)
    prepare(1)
    prepare(2)
    prepare(3)
    matrix_load.wait()
    for g in range(8):
        transform(g, 0)
    for g in range(8):
        transform(g, 1)
    lane = lax.broadcasted_iota(jnp.int32, (4, 128), 1)
    image = lax.broadcasted_iota(jnp.int32, (4, 128), 0)
    sums = jnp.sum(square_ref[...], axis=1, keepdims=True)
    sums = jnp.sum(jnp.where(lane == image, sums, 0.0), axis=0, keepdims=True)
    high = sums.astype(jnp.bfloat16).astype(jnp.float32)
    tail = jnp.concatenate([high, sums - high], axis=0).astype(jnp.bfloat16)

    order_load.wait()

    def send(part):
        rows = pl.ds(part * 32, 32)
        return pltpu.make_async_copy(message_ref.at[rows], out_ref.at[rows], out_sems.at[part])

    for part in range(4):

        def place(d, carry):
            for u in range(4):
                p = order_ref[d * 4 + u]
                at = pl.multiple_of((p & 15) * 768 + lax.shift_right_logical(p, 4) * 24, 8)
                message_ref[d, u * 8 : u * 8 + 8, :, :] = natural_ref[pl.ds(at, 16), :].astype(jnp.bfloat16).reshape(8, 2, 128)
            message_ref[d, 32, :, :] = tail
            return carry

        lax.fori_loop(part * 32, part * 32 + 32, place, 0, unroll=8)
        send(part).start()
    for part in range(4):
        send(part).wait()


def fourier(pair_order, images, matrix):
    return pl.pallas_call(
        fourier_kernel,
        out_shape=jax.ShapeDtypeStruct((128, 33, 2, 128), jnp.bfloat16),
        in_specs=[
            pl.BlockSpec(memory_space=pl.ANY),
            pl.BlockSpec(memory_space=pl.ANY),
            pl.BlockSpec(memory_space=pl.ANY),
        ],
        out_specs=pl.BlockSpec(memory_space=pl.ANY),
        scratch_shapes=[
            pltpu.SMEM((512,), jnp.int32),
            pltpu.VMEM((4, 128, 4096), jnp.float32),
            pltpu.VMEM((8, 512, 512), jnp.bfloat16),
            pltpu.VMEM((8, 256, 1024), jnp.bfloat16),
            pltpu.VMEM((8, 256, 1024), jnp.bfloat16),
            pltpu.VMEM((12288, 128), jnp.float32),
            pltpu.VMEM((4, 128), jnp.float32),
            pltpu.VMEM((128, 33, 2, 128), jnp.bfloat16),
            pltpu.SemaphoreType.DMA((4, 8)),
            pltpu.SemaphoreType.DMA,
            pltpu.SemaphoreType.DMA,
            pltpu.SemaphoreType.DMA((4,)),
        ],
        compiler_params=pltpu.CompilerParams(vmem_limit_bytes=60 << 20),
        cost_estimate=pl.CostEstimate(flops=4 << 30, bytes_accessed=14 << 20, transcendentals=0),
    )(pair_order, images, matrix)


PIECES = 4


def legendre_kernel(mine_ref, got_ref, legendre_ref, out_ref, weight_ref, column_ref, series_ref, in_sems, out_sems):
    def loads(slot):
        for piece in range(PIECES):
            rows = pl.ds(piece * 256, 257 if piece == PIECES - 1 else 256)
            yield pltpu.make_async_copy(legendre_ref.at[slot, rows], weight_ref.at[slot, rows], in_sems.at[slot, piece])

    def begin(slot):
        for copy in loads(slot):
            copy.start()

    begin(0)
    lanes = lax.broadcasted_iota(jnp.int32, (8, 128), 1)
    images = lax.broadcasted_iota(jnp.int32, (8, 128), 0) & 3
    scales = []
    for block in range(8):
        total = got_ref[block * 16, 32, :, :].astype(jnp.float32)
        for band in range(1, 16):
            total = total + got_ref[block * 16 + band, 32, :, :].astype(jnp.float32)
        both = jnp.broadcast_to(total[0:1] + total[1:2], (8, 128))
        whole = jnp.sum(jnp.where(lanes == images, both, 0.0), axis=1, keepdims=True)
        scales.append(1.0 / jnp.sqrt(whole / 8388608.0 + 1e-6))
    for slot in range(4):
        for band in range(16):
            for block in range(8):
                column_ref[slot, block * 16 : block * 16 + 16, band * 128 : band * 128 + 128] = got_ref[
                    block * 16 + band, slot * 8 : slot * 8 + 8, :, :
                ].reshape(16, 128)
    begin(1)

    def store(slot):
        return pltpu.make_async_copy(series_ref.at[slot], out_ref.at[slot], out_sems.at[slot])

    def work(slot, carry):
        @pl.when(slot < 2)
        def _():
            begin(slot + 2)

        for copy in loads(slot):
            copy.wait()
        product = lax.dot_general(weight_ref[slot], column_ref[slot], NT, preferred_element_type=jnp.float32)
        turned = jnp.transpose(product)
        keep = lax.broadcasted_iota(jnp.int32, (8, 1025), 1) <= 1023 - mine_ref[slot]
        for block in range(8):
            kept = jnp.where(keep, turned[block * 16 : block * 16 + 8], turned[block * 16 + 8 : block * 16 + 16])
            kept = kept * scales[block]
            series_ref[slot, block * 4 : block * 4 + 4, :] = kept[:4]
            series_ref[slot, 32 + block * 4 : 32 + block * 4 + 4, :] = kept[4:]
        store(slot).start()
        return carry

    lax.fori_loop(0, 4, work, 0)
    for slot in range(4):
        store(slot).wait()


def associated(mine, got, legendre):
    return pl.pallas_call(
        legendre_kernel,
        out_shape=jax.ShapeDtypeStruct((4, 64, 1025), jnp.float32),
        in_specs=[
            pl.BlockSpec(memory_space=pltpu.SMEM),
            pl.BlockSpec(memory_space=pltpu.VMEM),
            pl.BlockSpec(memory_space=pl.ANY),
        ],
        out_specs=pl.BlockSpec(memory_space=pl.ANY),
        scratch_shapes=[
            pltpu.VMEM((4, 1025, 2048), jnp.bfloat16),
            pltpu.VMEM((4, 128, 2048), jnp.bfloat16),
            pltpu.VMEM((4, 64, 1025), jnp.float32),
            pltpu.SemaphoreType.DMA((4, PIECES)),
            pltpu.SemaphoreType.DMA((4,)),
        ],
        compiler_params=pltpu.CompilerParams(vmem_limit_bytes=48 << 20),
        cost_estimate=pl.CostEstimate(flops=4 << 30, bytes_accessed=22 << 20, transcendentals=0),
    )(mine, got, legendre)


def shards(images, pair_order, legendre):
    message = fourier(pair_order, images, jnp.asarray(tables()))
    axes = ("tm", "lata", "latb")
    got = lax.all_to_all(message, axes, split_axis=0, concat_axis=0, tiled=True)
    mine = lax.dynamic_slice_in_dim(pair_order, lax.axis_index(axes) * 4, 4)
    return jnp.transpose(associated(mine, got, legendre), (0, 2, 1))


def solution(mesh):
    in_specs = (P("tm", ("lata", "latb"), None), P(), P(("tm", "lata", "latb"), None, None))
    out_specs = P(("tm", "lata", "latb"), None, None)
    return jax.shard_map(shards, mesh=mesh, in_specs=in_specs, out_specs=out_specs, check_vma=False)
```

```python
import math

import jax
import jax.numpy as jnp
import numpy as np
from jax import lax
from jax.experimental import pallas as pl
from jax.experimental.pallas import tpu as pltpu
from jax.sharding import PartitionSpec as P

NT = (((1,), (1,)), ((), ()))


def tables():
    q = np.arange(32)
    k = np.arange(256)

    def rows(freq, sign):
        angle = 2.0 * np.pi / 4096.0 * ((freq[:, None] * k[None, :]) % 4096)
        c, s = np.cos(angle) / 64.0, np.sin(angle) / 64.0
        zero = np.zeros_like(c)
        if sign == 0:
            return np.concatenate([c, zero], 1), np.concatenate([-s, zero], 1)
        if sign == 8:
            return np.concatenate([zero, c], 1), np.concatenate([zero, -s], 1)
        return np.concatenate([c, sign * s], 1), np.concatenate([-s, sign * c], 1)

    groups = []
    for g in range(8):
        first = []
        for residue, sign in ((g, 1 if g else 0), (16 - g if g else 8, -1 if g else 8)):
            for high in (0, 1):
                first += list(rows(residue + 16 * (63 - q if high else q), sign))
        groups.append(np.concatenate(first, 0))
    whole = np.stack(groups).astype(np.float32)
    hi = whole.astype(jnp.bfloat16)
    lo = (whole - hi.astype(np.float32)).astype(jnp.bfloat16)
    return np.concatenate([hi, lo], 1)


def rfft(x):
    n = len(x)
    if n == 2:
        return [(x[0] + x[1], None), (x[0] - x[1], None)]
    even, odd = rfft(x[0::2]), rfft(x[1::2])
    out = [None] * (n // 2 + 1)
    out[0] = (even[0][0] + odd[0][0], None)
    out[n // 2] = (even[0][0] - odd[0][0], None)
    for b in range(1, n // 4 + 1):
        er, ei = even[b]
        dr, di = odd[b]
        if 4 * b == n:
            out[b] = (er, -dr)
            continue
        c, s = math.cos(2 * math.pi * b / n), -math.sin(2 * math.pi * b / n)
        if 8 * b == n:
            tr, ti = (dr + di) * c, (di - dr) * c
        else:
            tr, ti = dr * c - di * s, dr * s + di * c
        out[b] = (er + tr, ei + ti)
        out[n // 2 - b] = (er - tr, ti - ei)
    return out


STRIDE = 16


def natural_row(p_low):
    return p_low * 16 if STRIDE == 256 else p_low * 512


def fourier_kernel(
    pair_ref, image_ref, matrix_ref, out_ref, order_ref, field_ref, rows_ref, za_ref, zb_ref, natural_ref, square_ref, message_ref, in_sems, row_sem, order_sem, out_sems
):
    z_refs = (za_ref, zb_ref)

    def load(image, piece):
        rows = pl.ds(pl.multiple_of(piece * 16, 16), 16)
        return pltpu.make_async_copy(image_ref.at[image, rows], field_ref.at[image, rows], in_sems.at[image, piece])

    def begin(image):
        for piece in range(8):
            load(image, piece).start()

    matrix_load = pltpu.make_async_copy(matrix_ref, rows_ref, row_sem)

    def prepare(image):
        z_ref = z_refs[image // 2]

        def piece(i, total):
            load(image, i).wait()
            at = pl.ds(pl.multiple_of(i * 16, 16), 16)
            to = pl.ds(pl.multiple_of(image % 2 * 128 + i * 16, 16), 16)
            for half in range(2):
                x = [field_ref[image, at, b * 256 + half * 128 : b * 256 + half * 128 + 128] for b in range(16)]
                squares = [v * v for v in x]
                while len(squares) > 1:
                    squares = [u + v for u, v in zip(squares[0::2], squares[1::2])]
                total = total + squares[0]
                bins = rfft(x)
                pairs = [(bins[0][0], bins[8][0])] + bins[1:8]
                for g in range(8):
                    for part in range(2):
                        value = pairs[g][part]
                        hi = value.astype(jnp.bfloat16)
                        lo = (value - hi.astype(jnp.float32)).astype(jnp.bfloat16)
                        lane = part * 256 + half * 128
                        z_ref[g, to, lane : lane + 128] = hi
                        z_ref[g, to, 512 + lane : 512 + lane + 128] = lo
            return total

        total = lax.fori_loop(0, 8, piece, jnp.zeros((16, 128), jnp.float32), unroll=2)
        square_ref[image : image + 1, :] = jnp.sum(total, axis=0, keepdims=True)

    def transform(g, unit):
        z_ref = z_refs[unit]
        both = lax.dot_general(rows_ref[g], z_ref[g, :, :512], NT, preferred_element_type=jnp.float32)
        rest = lax.dot_general(rows_ref[g, :256], z_ref[g, :, 512:], NT, preferred_element_type=jnp.float32)
        got = both[:256] + (both[256:] + rest)
        for which, residue in enumerate((g, 16 - g if g else 8)):
            for w in range(2):
                low = 15 - residue if w else residue
                for c in range(2):
                    first = ((which * 2 + w) * 2 + c) * 32
                    for t in range(2):
                        row = low * 768 + w * 8 + c * 4 + unit * 2 + t
                        natural_ref[pl.ds(row, 32, stride=24), :] = got[first : first + 32, t * 128 : t * 128 + 128]

    for image in range(4):
        begin(image)
    matrix_load.start()
    order_load = pltpu.make_async_copy(pair_ref, order_ref, order_sem)
    order_load.start()
    prepare(0)
    prepare(1)
    prepare(2)
    prepare(3)
    matrix_load.wait()
    for g in range(8):
        transform(g, 0)
    for g in range(8):
        transform(g, 1)
    lane = lax.broadcasted_iota(jnp.int32, (4, 128), 1)
    image = lax.broadcasted_iota(jnp.int32, (4, 128), 0)
    sums = jnp.sum(square_ref[...], axis=1, keepdims=True)
    sums = jnp.sum(jnp.where(lane == image, sums, 0.0), axis=0, keepdims=True)
    high = sums.astype(jnp.bfloat16).astype(jnp.float32)
    tail = jnp.concatenate([high, sums - high], axis=0).astype(jnp.bfloat16)

    order_load.wait()

    def send(part):
        rows = pl.ds(part * 32, 32)
        return pltpu.make_async_copy(message_ref.at[rows], out_ref.at[rows], out_sems.at[part])

    for part in range(4):

        def place(d, carry):
            for u in range(4):
                p = order_ref[d * 4 + u]
                at = pl.multiple_of((p & 15) * 768 + lax.shift_right_logical(p, 4) * 24, 8)
                message_ref[d, u * 8 : u * 8 + 8, :, :] = natural_ref[pl.ds(at, 16), :].astype(jnp.bfloat16).reshape(8, 2, 128)
            message_ref[d, 32, :, :] = tail
            return carry

        lax.fori_loop(part * 32, part * 32 + 32, place, 0, unroll=8)
        send(part).start()
    for part in range(4):
        send(part).wait()


def fourier(pair_order, images, matrix):
    return pl.pallas_call(
        fourier_kernel,
        out_shape=jax.ShapeDtypeStruct((128, 33, 2, 128), jnp.bfloat16),
        in_specs=[
            pl.BlockSpec(memory_space=pl.ANY),
            pl.BlockSpec(memory_space=pl.ANY),
            pl.BlockSpec(memory_space=pl.ANY),
        ],
        out_specs=pl.BlockSpec(memory_space=pl.ANY),
        scratch_shapes=[
            pltpu.SMEM((512,), jnp.int32),
            pltpu.VMEM((4, 128, 4096), jnp.float32),
            pltpu.VMEM((8, 512, 512), jnp.bfloat16),
            pltpu.VMEM((8, 256, 1024), jnp.bfloat16),
            pltpu.VMEM((8, 256, 1024), jnp.bfloat16),
            pltpu.VMEM((12288, 128), jnp.float32),
            pltpu.VMEM((4, 128), jnp.float32),
            pltpu.VMEM((128, 33, 2, 128), jnp.bfloat16),
            pltpu.SemaphoreType.DMA((4, 8)),
            pltpu.SemaphoreType.DMA,
            pltpu.SemaphoreType.DMA,
            pltpu.SemaphoreType.DMA((4,)),
        ],
        compiler_params=pltpu.CompilerParams(vmem_limit_bytes=60 << 20),
        cost_estimate=pl.CostEstimate(flops=4 << 30, bytes_accessed=14 << 20, transcendentals=0),
    )(pair_order, images, matrix)


PIECES = 4


def legendre_kernel(pairs_ref, got_ref, legendre_ref, out_ref, mine_ref, weight_ref, column_ref, series_ref, mine_sem, in_sems, out_sems):
    def loads(slot):
        for piece in range(PIECES):
            rows = pl.ds(piece * 256, 257 if piece == PIECES - 1 else 256)
            yield pltpu.make_async_copy(legendre_ref.at[slot, rows], weight_ref.at[slot, rows], in_sems.at[slot, piece])

    def begin(slot):
        for copy in loads(slot):
            copy.start()

    begin(0)
    mine_load = pltpu.make_async_copy(pairs_ref, mine_ref, mine_sem)
    mine_load.start()
    lanes = lax.broadcasted_iota(jnp.int32, (8, 128), 1)
    images = lax.broadcasted_iota(jnp.int32, (8, 128), 0) & 3
    scales = []
    for block in range(8):
        total = got_ref[block * 16, 32, :, :].astype(jnp.float32)
        for band in range(1, 16):
            total = total + got_ref[block * 16 + band, 32, :, :].astype(jnp.float32)
        both = jnp.broadcast_to(total[0:1] + total[1:2], (8, 128))
        whole = jnp.sum(jnp.where(lanes == images, both, 0.0), axis=1, keepdims=True)
        scales.append(1.0 / jnp.sqrt(whole / 8388608.0 + 1e-6))
    for slot in range(4):
        for band in range(16):
            for block in range(8):
                column_ref[slot, block * 16 : block * 16 + 16, band * 128 : band * 128 + 128] = got_ref[
                    block * 16 + band, slot * 8 : slot * 8 + 8, :, :
                ].reshape(16, 128)
    begin(1)

    def store(slot):
        return pltpu.make_async_copy(series_ref.at[slot], out_ref.at[slot], out_sems.at[slot])

    def work(slot, carry):
        @pl.when(slot < 2)
        def _():
            begin(slot + 2)

        for copy in loads(slot):
            copy.wait()
        product = lax.dot_general(weight_ref[slot], column_ref[slot], NT, preferred_element_type=jnp.float32)
        turned = jnp.transpose(product)
        keep = lax.broadcasted_iota(jnp.int32, (8, 1025), 1) <= 1023 - mine_ref[slot]
        for block in range(8):
            kept = jnp.where(keep, turned[block * 16 : block * 16 + 8], turned[block * 16 + 8 : block * 16 + 16])
            kept = kept * scales[block]
            series_ref[slot, block * 4 : block * 4 + 4, :] = kept[:4]
            series_ref[slot, 32 + block * 4 : 32 + block * 4 + 4, :] = kept[4:]
        store(slot).start()
        return carry

    mine_load.wait()
    lax.fori_loop(0, 4, work, 0)
    for slot in range(4):
        store(slot).wait()


def associated(mine, got, legendre):
    return pl.pallas_call(
        legendre_kernel,
        out_shape=jax.ShapeDtypeStruct((4, 64, 1025), jnp.float32),
        in_specs=[
            pl.BlockSpec(memory_space=pl.ANY),
            pl.BlockSpec(memory_space=pltpu.VMEM),
            pl.BlockSpec(memory_space=pl.ANY),
        ],
        out_specs=pl.BlockSpec(memory_space=pl.ANY),
        scratch_shapes=[
            pltpu.SMEM((4,), jnp.int32),
            pltpu.VMEM((4, 1025, 2048), jnp.bfloat16),
            pltpu.VMEM((4, 128, 2048), jnp.bfloat16),
            pltpu.VMEM((4, 64, 1025), jnp.float32),
            pltpu.SemaphoreType.DMA,
            pltpu.SemaphoreType.DMA((4, PIECES)),
            pltpu.SemaphoreType.DMA((4,)),
        ],
        compiler_params=pltpu.CompilerParams(vmem_limit_bytes=48 << 20),
        cost_estimate=pl.CostEstimate(flops=4 << 30, bytes_accessed=22 << 20, transcendentals=0),
    )(mine, got, legendre)


def shards(images, pair_order, legendre):
    message = fourier(pair_order, images, jnp.asarray(tables()))
    axes = ("tm", "lata", "latb")
    got = lax.all_to_all(message, axes, split_axis=0, concat_axis=0, tiled=True)
    mine = lax.dynamic_slice_in_dim(pair_order, lax.axis_index(axes) * 4, 4)
    return jnp.transpose(associated(mine, got, legendre), (0, 2, 1))


def solution(mesh):
    in_specs = (P("tm", ("lata", "latb"), None), P(), P(("tm", "lata", "latb"), None, None))
    out_specs = P(("tm", "lata", "latb"), None, None)
    return jax.shard_map(shards, mesh=mesh, in_specs=in_specs, out_specs=out_specs, check_vma=False)
```
